128 devices in a mesh: ctx: 32 (over x, z, core), head: 4 (over y).
Axes of the slice: x: 4, y: 4, z: 4, core: 2. Of those that a mesh axis runs over, the one named last changes fastest.
Arguments:
- queries: bfloat16 [1024, 4, 16, 128], P('ctx', 'head'), may hold values from -5 to 5
- new_keys: bfloat16 [1024, 4, 128], P('ctx', 'head'), may hold values from -5 to 5
- new_values: bfloat16 [1024, 4, 128], P('ctx', 'head'), may hold values from -6 to 6
- cache_keys: bfloat16 [65536, 4, 128], P('ctx', 'head'), may hold values from -6 to 6
- cache_values: bfloat16 [65536, 4, 128], P('ctx', 'head'), may hold values from -6 to 6
- hist_len: int32 [4], replicated, may hold values from 1 to 16384, 32768 in all
- new_count: int32 [4], replicated, may hold values from 1 to 256, 768 in all
- placement: int32 [512], P('ctx'), may hold values from 0 to 511, each once
Outputs:
- attended: bfloat16 [1024, 4, 16, 128], P(('ctx', 'head'))
The draws below stay inside these ranges and needn't reach their ends.
Inputs may be any that keep to these rules, and one draw needn't show every extreme that they name: `hist_len`: the four requests' histories sum to 32768; the longest is exactly 16384. `new_count`: the live new tokens sum to 768; the largest count is exactly 256. `placement`: each logical block is held by exactly one physical block.
All inputs are finite; a program needn't handle non-finite values.
Results may differ from the reference program's by a relative error of at most 0.0055.
Values may be sent and summed in bfloat16 or wider, within the bound.
No kernel may reach another device: no remote copies, remote signals or barrier semaphores. Data moves between devices by JAX's collectives and lax.ppermute only.
A program may use at most 320 MiB of HBM per device.

```python
import math
import jax
import jax.numpy as jnp
import numpy as np
from jax import lax

HD = 128
QPK = 16
REQ = 4
NEW = 256
BLK = 128
KVH = 4
NBLK = 512
SLOTS = 2048
BLOCKS_REQ = 128
CAP_REQ = 16384
HIST_TOTAL = 32768
NEW_TOTAL = 768
TOKENS = 1024
QT = 32
N_CTX = 32


def draw_queries(key, part):
    key = jax.random.fold_in(key, 5)
    sample = jax.random.truncated_normal(key, -5.0, 5.0, (TOKENS, KVH, QPK, HD), jnp.float32)
    return sample.astype(jnp.bfloat16)


def draw_new_keys(key, part):
    key = jax.random.fold_in(key, 9)
    sample = jax.random.truncated_normal(key, -5.0, 5.0, (TOKENS, KVH, HD), jnp.float32)
    return sample.astype(jnp.bfloat16)


def block_levels(own_key, dims, shards, least, largest):
    def one(dim, parts):
        steps = jax.random.uniform(jax.random.fold_in(jax.random.fold_in(own_key, 6), dim), (parts,), jnp.float32, least / len(shards), largest / len(shards))
        return jnp.repeat(jnp.exp(steps), dims[dim] // parts).reshape((-1,) + (1,) * (len(dims) - dim - 1))

    factor_of = one(*shards[0])
    for cut in shards[1:]:
        factor_of = factor_of * one(*cut)
    return factor_of


def length_profile(count, total, reach, skew):
    portions = [(1 << 20) // math.isqrt(standing ** skew) + 1 for standing in range(2, count + 1)]
    surplus, holding = total - reach - (count - 1), [1] * (count - 1)
    while surplus > 0:
        free = [i for i in range(count - 1) if holding[i] < reach]
        mass, budget = sum([portions[i] for i in free]), surplus
        for i in free:
            extra = min(reach - holding[i], max(1, budget * portions[i] // mass), surplus)
            holding[i] = holding[i] + extra
            surplus = surplus - extra
    return np.array([reach] + holding)


def ragged(rng, count, total, limit, lean):
    if count == 2:
        one = jax.random.randint(rng, (), max(1, total - limit), min(limit, total - 1) + 1)
        return jnp.stack([one, total - one])
    lengths = jnp.asarray(length_profile(count, total, limit, lean), jnp.int32)
    pairs = (count - 1) // 2
    donor, sink = lengths[1:1 + 2 * pairs:2], lengths[2:2 + 2 * pairs:2]
    slack = jnp.minimum(donor - 1, limit - sink)
    shifted = jax.random.randint(jax.random.fold_in(rng, 1), (pairs,), 0, 1 << 20) % (slack + 1)
    lengths = lengths.at[1:1 + 2 * pairs:2].set(donor - shifted).at[2:2 + 2 * pairs:2].set(sink + shifted)
    return lengths[jax.random.permutation(jax.random.fold_in(rng, 2), count)]


def bell_draw(key, shape, deviation, reach, shards=(), kind=jnp.bfloat16):
    entries = jax.random.normal(key, shape, jnp.float32) * deviation
    if len(shards) > 0:
        entries = block_levels(key, shape, shards, -0.22, 0.18) * entries
    return jnp.clip(entries, min=-reach, max=reach).astype(kind)


def setup_inputs(seed: int = 0) -> dict:
    splits = jax.random.split(jax.random.key(seed), 9)
    queries = draw_queries(jax.random.fold_in(splits[8], 71), 0)
    new_keys = draw_new_keys(jax.random.fold_in(splits[8], 71), 0)
    new_values = bell_draw(splits[2], (TOKENS, KVH, HD), 1.0, 6.0, ((0, 32), (1, 4)))
    cache_keys = bell_draw(splits[3], (NBLK * BLK, KVH, HD), 1.0, 6.0, ((0, 32), (1, 4)))
    cache_values = bell_draw(splits[4], (NBLK * BLK, KVH, HD), 1.0, 6.0, ((0, 32), (1, 4)))
    hist_len = ragged(splits[5], REQ, HIST_TOTAL, CAP_REQ, 2).astype(jnp.int32)
    new_count = ragged(splits[6], REQ, NEW_TOTAL, NEW, 1).astype(jnp.int32)
    placement = jax.random.permutation(splits[7], NBLK).astype(jnp.int32)
    return {"queries": queries, "new_keys": new_keys, "new_values": new_values, "cache_keys": cache_keys, "cache_values": cache_values, "hist_len": hist_len, "new_count": new_count, "placement": placement}


masked_value = -1e+30

def lookup(table, indices):
    matches = indices[:, None] == jnp.arange(table.shape[0], dtype=jnp.int32)[None, :]
    return lax.optimization_barrier(jnp.sum(jnp.where(matches, table[None, :], 0), axis=1)).astype(jnp.int32)

def token_meta(first_row, row_count, hist_len, new_count, dead_mark):
    tokens = first_row + jnp.arange(row_count, dtype=jnp.int32)
    request = tokens // NEW
    offset = tokens % NEW
    position = lookup(hist_len, request) + offset
    is_live = offset < lookup(new_count, request)
    return (jnp.where(is_live, request, dead_mark).astype(jnp.int32), position.astype(jnp.int32))

def cache_meta(block_ids, blocks_req, hist_len):
    logical = jnp.repeat(block_ids, BLK)
    in_block = jnp.arange(logical.shape[0], dtype=jnp.int32) % BLK
    request = logical // blocks_req
    position = logical % blocks_req * BLK + in_block
    is_live = position < lookup(hist_len, request)
    return (jnp.where(is_live, request, -1).astype(jnp.int32), position.astype(jnp.int32))

def reference(queries, new_keys, new_values, cache_keys, cache_values, hist_len, new_count, placement):
    score_scale = 1.0 / math.sqrt(HD)
    query_req, query_pos = token_meta(0, TOKENS, hist_len, new_count, -2)
    cache_req, cache_pos = cache_meta(placement, BLOCKS_REQ, hist_len)
    fresh_req, fresh_pos = token_meta(0, TOKENS, hist_len, new_count, -1)
    query_heads = jnp.moveaxis(queries, 1, 0).astype(jnp.float32)

    def shard_step(state_now, shard_index):
        highest, numerator, denominator = state_now
        slot_first = (shard_index * SLOTS).astype(jnp.int32)
        token_first = (shard_index * QT).astype(jnp.int32)
        all_keys = jnp.concatenate([lax.dynamic_slice_in_dim(cache_keys, slot_first, SLOTS, 0), lax.dynamic_slice_in_dim(new_keys, token_first, QT, 0)], axis=0)
        all_values = jnp.concatenate([lax.dynamic_slice_in_dim(cache_values, slot_first, SLOTS, 0), lax.dynamic_slice_in_dim(new_values, token_first, QT, 0)], axis=0)
        key_req = jnp.concatenate([lax.dynamic_slice_in_dim(cache_req, slot_first, SLOTS, 0), lax.dynamic_slice_in_dim(fresh_req, token_first, QT, 0)], axis=0)
        key_pos = jnp.concatenate([lax.dynamic_slice_in_dim(cache_pos, slot_first, SLOTS, 0), lax.dynamic_slice_in_dim(fresh_pos, token_first, QT, 0)], axis=0)
        allowed = (query_req[:, None] == key_req[None, :]) & (key_pos[None, :] <= query_pos[:, None])
        allowed = allowed[:, None, :]

        def head_part(operands):
            query_one, key_one, value_one = operands
            scores = jnp.einsum('tqd,kd->tqk', query_one, key_one.astype(jnp.float32)) * score_scale
            row_top = lax.optimization_barrier(jnp.max(jnp.where(allowed, scores, masked_value), axis=-1))
            weights = jnp.where(allowed, jnp.exp(scores - row_top[..., None]), 0.0)
            totals = lax.optimization_barrier(jnp.sum(weights, axis=-1))
            weights_b = lax.optimization_barrier(weights.astype(jnp.bfloat16))
            summed = jnp.einsum('tqk,kd->tqd', weights_b.astype(jnp.float32), value_one.astype(jnp.float32))
            return (summed.astype(jnp.bfloat16), row_top, totals)
        summed, row_top, totals = lax.map(head_part, (query_heads, jnp.moveaxis(all_keys, 1, 0), jnp.moveaxis(all_values, 1, 0)))
        summed = lax.optimization_barrier(summed)
        new_high = jnp.maximum(highest, row_top)
        old_weight = jnp.exp(highest - new_high)
        new_weight = jnp.exp(row_top - new_high)
        numerator = numerator * old_weight[..., None] + new_weight[..., None] * summed.astype(jnp.float32)
        denominator = denominator * old_weight + new_weight * totals
        return ((new_high, numerator, denominator), None)
    start_state = (jnp.full((KVH, TOKENS, QPK), masked_value, jnp.float32), jnp.zeros((KVH, TOKENS, QPK, HD), jnp.float32), jnp.zeros((KVH, TOKENS, QPK), jnp.float32))
    final_state, _ = lax.scan(shard_step, start_state, jnp.arange(N_CTX, dtype=jnp.int32))
    highest, numerator, denominator = final_state
    attended = (numerator / jnp.maximum(denominator, 1.0)[..., None]).astype(jnp.bfloat16)
    return jnp.moveaxis(attended, 0, 1)
```

```python
import functools
import math

import jax
import jax.numpy as jnp
import numpy as np
from jax import lax
from jax.experimental import pallas as pl
from jax.experimental.pallas import tpu as pltpu
from jax.sharding import Mesh, PartitionSpec as P

HD = 128
QPK = 16
REQ = 4
NEW = 256
BLK = 128
QT = 32
HERE = 16
PEERS = 8
PIECE = QT * QPK
ROWS = NEW * QPK
CHUNK = 128
CHUNKS = ROWS // CHUNK
STAT = 16
BLOCKS_REQ = 128
CAP = 9
RELAY = 5
TILE = 1024
TILES = ROWS // TILE
SUB = 256
FIRST = 1024
CB = 4
AUG = HD + STAT

masked_value = -1e30
SCALE = 1.0 / math.sqrt(HD)
SCALE2 = SCALE * math.log2(math.e)

VMEM = pl.BlockSpec(memory_space=pltpu.VMEM)
SMEM = pl.BlockSpec(memory_space=pltpu.SMEM)
f32, bf16, i32 = jnp.float32, jnp.bfloat16, jnp.int32


def block_state(placement, hist_len, i):
    logical = placement[i]
    request = logical // BLOCKS_REQ
    live = hist_len[request] - (logical % BLOCKS_REQ) * BLK
    return request, jnp.clip(live, 0, BLK)


def rows_at(first, count):
    return pl.ds(pl.multiple_of(first, BLK), count)


def pack_kernel(cap, relay, me, placement, hist_len, keys, values, up, down):
    state = []
    count = [jnp.int32(0)] * REQ
    for i in range(HERE):
        request, live = block_state(placement, hist_len, i)
        away = jnp.where(live > 0, (request - me[0] + REQ) % REQ, 0)
        state.append((away, live, [count[d] for d in range(REQ)]))
        count = [count[d] + (away == d).astype(i32) for d in range(REQ)]
    up_room = jnp.minimum(relay, jnp.maximum(cap - count[1], 0))
    down_room = jnp.minimum(relay, jnp.maximum(cap - count[3], 0))
    far_up = jnp.minimum(jnp.maximum((count[2] + 1) // 2, count[2] - down_room), up_room)
    over = (count[1] > cap) | (count[3] > cap) | (count[2] > up_room + down_room)
    part = {d: (jnp.int32(0), jnp.int32(0)) for d in ("near up", "near down", "far up", "far down")}
    for i, (away, live, before) in enumerate(state):
        src = slice(i * BLK, (i + 1) * BLK)
        goes_up = before[2] < far_up
        far_down = before[2] - far_up
        places = (
            ("near up", up, away == 1, before[1], before[1], cap),
            ("near down", down, away == 3, before[3], before[3], cap),
            ("far up", up, (away == 2) & goes_up, before[2], cap - 1 - before[2], relay),
            ("far down", down, (away == 2) & ~goes_up, far_down, cap - 1 - far_down, down_room),
        )
        for name, send, hit, order, slot, room in places:

            @pl.when(hit & (order < room))
            def _(send=send, slot=slot, src=src):
                send[rows_at(slot * (2 * BLK), BLK), :] = keys[src, :]
                send[rows_at(slot * (2 * BLK) + BLK, BLK), :] = values[src, :]

            partly = hit & (live < BLK)
            part[name] = tuple(jnp.where(partly, new, old) for new, old in zip((order, live), part[name]))
    lane = lax.broadcasted_iota(i32, (STAT, HD), 1)
    numbers = (
        (up, jnp.minimum(count[1], cap), "near up", far_up, "far up"),
        (down, jnp.minimum(count[3], cap), "near down", jnp.minimum(count[2] - far_up, down_room), "far down"),
    )
    for send, near, near_name, far, far_name in numbers:
        meta = jnp.zeros((STAT, HD), i32)
        for k, number in enumerate((near, *part[near_name], over.astype(i32), far, *part[far_name])):
            meta = jnp.where(lane == k, number, meta)
        send[2 * cap * BLK :, :] = meta.astype(f32).astype(bf16)


def split3(x):
    hi = x.astype(bf16).astype(f32)
    mid = (x - hi).astype(bf16).astype(f32)
    lo = (x - hi - mid).astype(bf16).astype(f32)
    return [hi, mid, lo]


def put(k_all, v_all, k_block, v_block, slot):
    at = rows_at(slot * BLK, BLK)
    k_all[at, :] = k_block
    v_all[0:HD, at] = jnp.transpose(v_block.astype(f32)).astype(bf16)
    v_all[HD:, at] = jnp.where(lax.broadcasted_iota(i32, (STAT, BLK), 0) == 0, 1.0, 0.0).astype(bf16)


def trim(k_all, v_all, slot, live):
    at = rows_at(slot * BLK, BLK)
    k32 = k_all[at, :].astype(f32)
    k_all[at, :] = jnp.where(lax.broadcasted_iota(i32, (BLK, HD), 0) < live, k32, k32[0:1, :]).astype(bf16)
    v32 = v_all[:, at].astype(f32)
    v_all[:, at] = jnp.where(lax.broadcasted_iota(i32, (AUG, BLK), 1) < live, v32, 0.0).astype(bf16)


def fill(k_all, v_all, count):
    chunks = (count + CB - 1) // CB

    def again(i, _):
        k_all[rows_at(i * BLK, BLK), :] = k_all[rows_at((count - 1) * BLK, BLK), :]
        v_all[:, rows_at(i * BLK, BLK)] = jnp.zeros((AUG, BLK), bf16)
        return 0

    lax.fori_loop(count, chunks * CB, again, 0)
    return chunks


BY_HEAD = (((1,), (1,)), ((), ()))
BY_KEY = (((1,), (0,)), ((), ()))


def flash(begin, end, tiles, q, k_all, v_all, acc, tops, scores, found):
    wide = CB * BLK
    total = (end - begin) * tiles

    def make(c, t, n, u):
        cut = slice(u * SUB, (u + 1) * SUB)
        s = lax.dot_general(
            k_all[rows_at(c * wide, wide), :],
            q[rows_at(t * TILE + u * SUB, SUB), :],
            BY_HEAD,
            preferred_element_type=f32,
        )
        scores[n][:, cut] = s
        found[n][0:1, cut] = jnp.max(s, axis=0, keepdims=True)

    def weigh(c, t, n, u):
        cut = slice(u * SUB, (u + 1) * SUB)
        at = rows_at(t * TILE + u * SUB, SUB)
        old = tops[0:1, at]
        top = jnp.maximum(old, found[n][0:1, cut])
        w = jnp.exp2((scores[n][:, cut] - top) * SCALE2).astype(bf16)
        keep = jnp.exp2((old - top) * SCALE2)
        tops[0:1, at] = top
        acc[:, at] = acc[:, at] * keep + lax.dot_general(
            v_all[:, rows_at(c * wide, wide)], w, BY_KEY, preferred_element_type=f32
        )

    def after(c, t):
        wrap = t + 1 == tiles
        return jnp.minimum(c + wrap.astype(i32), end - 1), jnp.where(wrap, 0, t + 1)

    @pl.when(total > 0)
    def _():
        for u in range(TILE // SUB):
            make(begin, jnp.int32(0), 0, u)

        def pair(p, now):
            c, t = now
            c1, t1 = after(c, t)
            c2, t2 = after(c1, t1)
            for u in range(TILE // SUB):
                make(c1, t1, 1, u)
                weigh(c, t, 0, u)
            spare = jnp.where(2 * p + 1 < total, t1, TILES)
            for u in range(TILE // SUB):
                make(c2, t2, 0, u)
                weigh(c1, spare, 1, u)
            return c2, t2

        lax.fori_loop(0, (total + 1) // 2, pair, (begin, jnp.int32(0)))


def live_tiles(tokens):
    per = TILE // QPK
    return (tokens + per - 1) // per


def own_kernel(
    me, placement, hist_len, new_count, q_mine, q_theirs, new_keys, new_values, keys, values,
    q_all, acc, tops, k_all, v_all, counts, score0, score1, found0, found1,
):
    x, z, core = me[0], me[1], me[2]
    for n, shift in enumerate((0, 1, 3, 2)):
        place = ((z - shift + 4) % 4) * 2
        rows = slice(n * PIECE, (n + 1) * PIECE)
        q_all[rows_at((place + core) * PIECE, PIECE), :] = q_mine[rows, :]
        q_all[rows_at((place + 1 - core) * PIECE, PIECE), :] = q_theirs[rows, :]

    tokens = new_count[x]
    new_first = (z * 2 + core) * QT
    k_all[0:BLK, :] = jnp.zeros((BLK, HD), bf16)
    k_all[0:QT, :] = new_values[...]
    put(k_all, v_all, k_all[0:BLK, :], k_all[0:BLK, :], 0)
    for t in range(ROWS // FIRST):
        at = slice(t * FIRST, (t + 1) * FIRST)
        s = lax.dot_general(new_keys[...], q_all[at, :], BY_HEAD, preferred_element_type=f32)
        offset = lax.broadcasted_iota(i32, (QT, FIRST), 0)
        token = (t * FIRST + lax.broadcasted_iota(i32, (1, FIRST), 1)) // QPK
        allowed = offset <= jnp.minimum(token, tokens - 1) - new_first
        top = jnp.max(jnp.where(allowed, s, masked_value), axis=0, keepdims=True)
        w = jnp.where(allowed, jnp.exp2((s - top) * SCALE2), 0.0).astype(bf16)
        tops[0:1, at] = top
        acc[:, at] = lax.dot_general(v_all[:, 0:QT], w, BY_KEY, preferred_element_type=f32)

    def own(i, count):
        request, live = block_state(placement, hist_len, i)
        hit = (request == x) & (live > 0)

        @pl.when(hit)
        def _():
            at = rows_at(i * BLK, BLK)
            put(k_all, v_all, keys[at, :], values[at, :], count)

            @pl.when(live < BLK)
            def _():
                trim(k_all, v_all, count, live)

        return count + hit.astype(i32)

    count = lax.fori_loop(0, HERE, own, jnp.int32(0))
    counts[0] = count
    counts[1] = 0
    flash(
        jnp.int32(0), count // CB, live_tiles(tokens), q_all, k_all, v_all, acc, tops, (score0, score1), (found0, found1)
    )


def take(got, slots, last, count, k_all, v_all):
    lane = lax.broadcasted_iota(i32, (STAT, HD), 1)
    first = lax.broadcasted_iota(i32, (STAT, HD), 0) == 0
    meta = got[2 * slots * BLK :, :].astype(f32)
    here, part_at, part, over = (
        jnp.sum(jnp.where((lane == which) & first, meta, 0.0)).astype(i32)
        for which in ((4, 5, 6, 3) if last else (0, 1, 2, 3))
    )

    def two(i, _):
        for n in (2 * i, 2 * i + 1):
            n_at = jnp.minimum(n, slots - 1)
            at = (slots - 1 - n_at if last else n_at) * (2 * BLK)
            put(k_all, v_all, got[rows_at(at, BLK), :], got[rows_at(at + BLK, BLK), :], count + n)
        return 0

    lax.fori_loop(0, (here + 1) // 2, two, 0)

    @pl.when(part > 0)
    def _():
        trim(k_all, v_all, count + part_at, part)

    return count + here, over


def near_kernel(
    cap, me, new_count, counts, q, got1, got3, acc_in, tops_in, k_in, v_in,
    acc, tops, k_all, v_all, counts_out, score0, score1, found0, found1,
):
    begin = counts[0] // CB
    count, over1 = take(got1, cap, False, counts[0], k_all, v_all)
    count, over3 = take(got3, cap, False, count, k_all, v_all)
    counts_out[0] = count
    counts_out[1] = jnp.maximum(over1, over3)
    flash(
        begin, count // CB, live_tiles(new_count[me[0]]), q, k_all, v_all, acc, tops, (score0, score1), (found0, found1)
    )


def far_kernel(
    relay, me, new_count, counts, q, far1, far3, acc_in, tops_in, k_in, v_in,
    acc, tops, k_all, v_all, out, score0, score1, found0, found1,
):
    begin = counts[0] // CB
    count, over1 = take(far1, relay, True, counts[0], k_all, v_all)
    count, over3 = take(far3, relay, True, count, k_all, v_all)
    end = fill(k_all, v_all, count)
    tokens = new_count[me[0]]
    flash(begin, end, live_tiles(tokens), q, k_all, v_all, acc, tops, (score0, score1), (found0, found1))
    live = lax.broadcasted_iota(i32, (1, ROWS), 1) // QPK < tokens
    flag = jnp.full((1, ROWS), jnp.maximum(counts[1], jnp.maximum(over1, over3)).astype(f32))
    top = jnp.where(live, tops[0:1, 0:ROWS] * SCALE, masked_value)
    total = jnp.where(live, acc[HD : HD + 1, 0:ROWS], 0.0)
    pad = jnp.zeros((STAT - 7, ROWS), f32)
    stat = jnp.concatenate(split3(top) + split3(total) + [flag, pad], axis=0).astype(bf16)
    for chunk in range(CHUNKS):
        at = slice(chunk * CHUNK, (chunk + 1) * CHUNK)
        out[chunk, 0:HD, :] = jnp.where(live[:, at], acc[0:HD, at], 0.0).astype(bf16)
        out[chunk, HD:, :] = stat[:, at]


def merge_kernel(got, out, flag):
    over = jnp.zeros((1, CHUNK), f32)
    for y in range(REQ):
        tops, totals = [], []
        for c in range(PEERS):
            stat = got[c * REQ + y, HD:, :].astype(f32)
            tops.append(stat[0:1] + stat[1:2] + stat[2:3])
            totals.append(stat[3:4] + stat[4:5] + stat[5:6])
            over = jnp.maximum(over, stat[6:7])
        top, total = jnp.concatenate(tops, axis=0), jnp.concatenate(totals, axis=0)
        rescale = jnp.exp(top - jnp.max(top, axis=0, keepdims=True))
        denominator = jnp.sum(rescale * total, axis=0, keepdims=True)
        share = rescale / jnp.maximum(denominator, 1.0)
        numerator = jnp.zeros((HD, CHUNK), f32)
        for c in range(PEERS):
            numerator = numerator + share[c : c + 1, :] * got[c * REQ + y, 0:HD, :].astype(f32)
        out[:, y] = jnp.transpose(numerator).astype(bf16).reshape(CHUNK // QPK, QPK, HD)
    flag[0] = jnp.max(over).astype(i32)


def shifted(x, axis, by):
    peers = lax.axis_size(axis)
    return lax.ppermute(x, axis, [(i, (i + by) % peers) for i in range(peers)])


def params(mib):
    return pltpu.CompilerParams(vmem_limit_bytes=mib * 1024 * 1024)


def gather_queries(q):
    mine = jnp.concatenate([q] + [shifted(q, "z", by) for by in (1, -1, 2)], axis=0)
    return mine, shifted(mine, "core", 1)


WORKING = [pltpu.VMEM((CB * BLK, TILE), f32)] * 2 + [pltpu.VMEM((8, TILE), f32)] * 2


def cost(blocks):
    return pl.CostEstimate(flops=blocks, bytes_accessed=blocks, transcendentals=0)


def run(cap, relay, me, q, new_keys, new_values, keys, values, hist_len, new_count, placement):
    size = 2 * cap * BLK + STAT
    up, down = pl.pallas_call(
        functools.partial(pack_kernel, cap, relay),
        out_shape=[jax.ShapeDtypeStruct((size, HD), bf16)] * 2,
        in_specs=[SMEM] * 3 + [VMEM] * 2,
        out_specs=[VMEM] * 2,
        compiler_params=params(24),
        name="pack",
    )(me, placement, hist_len, keys, values)
    got1, got3 = shifted(up, "x", 1), shifted(down, "x", -1)
    tail = 2 * (cap - relay) * BLK
    queries = gather_queries(q)
    held = (HERE + 2 * cap + 2 * relay + CB) * BLK
    state = [
        jax.ShapeDtypeStruct((AUG, ROWS + TILE), f32),
        jax.ShapeDtypeStruct((8, ROWS + TILE), f32),
        jax.ShapeDtypeStruct((held, HD), bf16),
        jax.ShapeDtypeStruct((AUG, held), bf16),
    ]
    two = jax.ShapeDtypeStruct((2,), i32)
    q, *now, counts = pl.pallas_call(
        own_kernel,
        out_shape=[jax.ShapeDtypeStruct((ROWS, HD), bf16)] + state + [two],
        in_specs=[SMEM] * 4 + [VMEM] * 6,
        out_specs=[VMEM] * 5 + [SMEM],
        scratch_shapes=WORKING,
        compiler_params=params(32),
        cost_estimate=cost(8),
        name="own",
    )(me, placement, hist_len, new_count, *queries, new_keys, new_values, keys, values)
    counts, got1, got3 = lax.optimization_barrier((counts, got1, got3))
    far1, far3 = shifted(got1[tail:], "x", 1), shifted(got3[tail:], "x", -1)
    *now, counts = pl.pallas_call(
        functools.partial(near_kernel, cap),
        out_shape=state + [two],
        in_specs=[SMEM] * 3 + [VMEM] * 7,
        out_specs=[VMEM] * 4 + [SMEM],
        input_output_aliases={6: 0, 7: 1, 8: 2, 9: 3},
        scratch_shapes=WORKING,
        compiler_params=params(32),
        cost_estimate=cost(8),
        name="near",
    )(me, new_count, counts, q, got1, got3, *now)
    *_, parts = pl.pallas_call(
        functools.partial(far_kernel, relay),
        out_shape=state + [jax.ShapeDtypeStruct((CHUNKS, CHUNK + STAT, HD), bf16)],
        in_specs=[SMEM] * 3 + [VMEM] * 7,
        out_specs=[VMEM] * 5,
        input_output_aliases={6: 0, 7: 1, 8: 2, 9: 3},
        scratch_shapes=WORKING,
        compiler_params=params(32),
        cost_estimate=cost(4),
        name="far",
    )(me, new_count, counts, q, far1, far3, *now)
    moved = lax.all_to_all(parts, ("z", "core", "head"), split_axis=0, concat_axis=0, tiled=True)
    return pl.pallas_call(
        merge_kernel,
        out_shape=[jax.ShapeDtypeStruct((CHUNK // QPK, REQ, QPK, HD), bf16), jax.ShapeDtypeStruct((1,), i32)],
        in_specs=[VMEM],
        out_specs=[VMEM, SMEM],
        compiler_params=params(24),
        name="merge",
    )(moved)


def local(queries, new_keys, new_values, cache_keys, cache_values, hist_len, new_count, placement):
    me = jnp.stack([lax.axis_index(a) for a in ("x", "z", "core")]).astype(i32)
    rows = queries.reshape(PIECE, HD)
    rest = (new_keys[:, 0], new_values[:, 0], cache_keys[:, 0], cache_values[:, 0], hist_len, new_count, placement)
    attended, flag = run(CAP, RELAY, me, rows, *rest)
    return lax.cond(flag[0] > 0, lambda: run(HERE, HERE, me, rows, *rest)[0], lambda: attended)


def solution(mesh):
    fine = Mesh(mesh.devices.reshape(4, 4, 2, 4), ("x", "z", "core", "head"))
    ctx = ("x", "z", "core")
    in_specs = (
        P(ctx, "head", None, None),
        P(ctx, "head", None),
        P(ctx, "head", None),
        P(ctx, "head", None),
        P(ctx, "head", None),
        P(),
        P(),
        P(ctx),
    )
    out_specs = P((*ctx, "head"), None, None, None)
    return jax.shard_map(local, mesh=fine, in_specs=in_specs, out_specs=out_specs, check_vma=False)
```

```python
import functools
import math

import jax
import jax.numpy as jnp
import numpy as np
from jax import lax
from jax.experimental import pallas as pl
from jax.experimental.pallas import tpu as pltpu
from jax.sharding import Mesh, PartitionSpec as P

HD = 128
QPK = 16
REQ = 4
NEW = 256
BLK = 128
QT = 32
HERE = 16
PEERS = 4
PIECE = QT * QPK
ROWS = NEW * QPK
CHUNK = 128
HALF = ROWS // 2
CHUNKS = HALF // CHUNK
STAT = 16
BLOCKS_REQ = 128
CAP = 9
RELAY = 5
TILE = 1024
TILES = ROWS // TILE
SUB = 256
FIRST = 1024
CB = 4
AUG = HD + STAT

masked_value = -1e30
SCALE = 1.0 / math.sqrt(HD)
SCALE2 = SCALE * math.log2(math.e)

VMEM = pl.BlockSpec(memory_space=pltpu.VMEM)
SMEM = pl.BlockSpec(memory_space=pltpu.SMEM)
f32, bf16, i32 = jnp.float32, jnp.bfloat16, jnp.int32


def block_state(placement, hist_len, i):
    logical = placement[i]
    request = logical // BLOCKS_REQ
    live = hist_len[request] - (logical % BLOCKS_REQ) * BLK
    return request, jnp.clip(live, 0, BLK)


def rows_at(first, count):
    return pl.ds(pl.multiple_of(first, BLK), count)


def pack_kernel(cap, relay, me, placement, hist_len, keys, values, up, down, over_out):
    state = []
    count = [jnp.int32(0)] * REQ
    for i in range(HERE):
        request, live = block_state(placement, hist_len, i)
        away = jnp.where(live > 0, (request - me[0] + REQ) % REQ, 0)
        state.append((away, live, [count[d] for d in range(REQ)]))
        count = [count[d] + (away == d).astype(i32) for d in range(REQ)]
    up_room = jnp.minimum(relay, jnp.maximum(cap - count[1], 0))
    down_room = jnp.minimum(relay, jnp.maximum(cap - count[3], 0))
    far_up = jnp.minimum(jnp.maximum((count[2] + 1) // 2, count[2] - down_room), up_room)
    over = (count[1] > cap) | (count[3] > cap) | (count[2] > up_room + down_room)
    over_out[0] = over.astype(i32)
    part = {d: (jnp.int32(0), jnp.int32(0)) for d in ("near up", "near down", "far up", "far down")}
    for i, (away, live, before) in enumerate(state):
        src = slice(i * BLK, (i + 1) * BLK)
        goes_up = before[2] < far_up
        far_down = before[2] - far_up
        places = (
            ("near up", up, away == 1, before[1], before[1], cap),
            ("near down", down, away == 3, before[3], before[3], cap),
            ("far up", up, (away == 2) & goes_up, before[2], cap - 1 - before[2], relay),
            ("far down", down, (away == 2) & ~goes_up, far_down, cap - 1 - far_down, down_room),
        )
        for name, send, hit, order, slot, room in places:

            @pl.when(hit & (order < room))
            def _(send=send, slot=slot, src=src):
                send[rows_at(slot * (2 * BLK), BLK), :] = keys[src, :]
                send[rows_at(slot * (2 * BLK) + BLK, BLK), :] = values[src, :]

            partly = hit & (live < BLK)
            part[name] = tuple(jnp.where(partly, new, old) for new, old in zip((order, live), part[name]))
    lane = lax.broadcasted_iota(i32, (STAT, HD), 1)
    numbers = (
        (up, jnp.minimum(count[1], cap), "near up", far_up, "far up"),
        (down, jnp.minimum(count[3], cap), "near down", jnp.minimum(count[2] - far_up, down_room), "far down"),
    )
    for send, near, near_name, far, far_name in numbers:
        meta = jnp.zeros((STAT, HD), i32)
        for k, number in enumerate((near, *part[near_name], over.astype(i32), far, *part[far_name])):
            meta = jnp.where(lane == k, number, meta)
        send[2 * cap * BLK :, :] = meta.astype(f32).astype(bf16)


def split3(x):
    hi = x.astype(bf16).astype(f32)
    mid = (x - hi).astype(bf16).astype(f32)
    lo = (x - hi - mid).astype(bf16).astype(f32)
    return [hi, mid, lo]


def put(k_all, v_all, k_block, v_block, slot):
    at = rows_at(slot * BLK, BLK)
    k_all[at, :] = k_block
    v_all[0:HD, at] = jnp.transpose(v_block.astype(f32)).astype(bf16)
    v_all[HD:, at] = jnp.where(lax.broadcasted_iota(i32, (STAT, BLK), 0) == 0, 1.0, 0.0).astype(bf16)


def trim(k_all, v_all, slot, live):
    at = rows_at(slot * BLK, BLK)
    k32 = k_all[at, :].astype(f32)
    k_all[at, :] = jnp.where(lax.broadcasted_iota(i32, (BLK, HD), 0) < live, k32, k32[0:1, :]).astype(bf16)
    v32 = v_all[:, at].astype(f32)
    v_all[:, at] = jnp.where(lax.broadcasted_iota(i32, (AUG, BLK), 1) < live, v32, 0.0).astype(bf16)


def fill(k_all, v_all, count):
    chunks = (count + CB - 1) // CB

    def again(i, _):
        k_all[rows_at(i * BLK, BLK), :] = k_all[rows_at((count - 1) * BLK, BLK), :]
        v_all[:, rows_at(i * BLK, BLK)] = jnp.zeros((AUG, BLK), bf16)
        return 0

    lax.fori_loop(count, chunks * CB, again, 0)
    return chunks


BY_HEAD = (((1,), (1,)), ((), ()))
BY_KEY = (((1,), (0,)), ((), ()))


def flash(begin, end, tiles, q, k_all, v_all, acc, tops, scores, found):
    wide = CB * BLK
    (first0, count0), (first1, count1) = tiles
    total = (end - begin) * (count0 + count1)

    def place(t):
        return jnp.where(t < count0, first0 + t, first1 + t - count0)

    def make(c, t, n, u):
        cut = slice(u * SUB, (u + 1) * SUB)
        s = lax.dot_general(
            k_all[rows_at(c * wide, wide), :],
            q[rows_at(place(t) * TILE + u * SUB, SUB), :],
            BY_HEAD,
            preferred_element_type=f32,
        )
        scores[n][:, cut] = s
        found[n][0:1, cut] = jnp.max(s, axis=0, keepdims=True)

    def weigh(c, t, n, u):
        cut = slice(u * SUB, (u + 1) * SUB)
        at = rows_at(t * TILE + u * SUB, SUB)
        old = tops[0:1, at]
        top = jnp.maximum(old, found[n][0:1, cut])
        w = jnp.exp2((scores[n][:, cut] - top) * SCALE2).astype(bf16)
        keep = jnp.exp2((old - top) * SCALE2)
        tops[0:1, at] = top
        acc[:, at] = acc[:, at] * keep + lax.dot_general(
            v_all[:, rows_at(c * wide, wide)], w, BY_KEY, preferred_element_type=f32
        )

    def after(c, t):
        wrap = t + 1 == count0 + count1
        return jnp.minimum(c + wrap.astype(i32), end - 1), jnp.where(wrap, 0, t + 1)

    @pl.when(total > 0)
    def _():
        for u in range(TILE // SUB):
            make(begin, jnp.int32(0), 0, u)

        def pair(p, now):
            c, t = now
            c1, t1 = after(c, t)
            c2, t2 = after(c1, t1)
            for u in range(TILE // SUB):
                make(c1, t1, 1, u)
                weigh(c, place(t), 0, u)
            spare = jnp.where(2 * p + 1 < total, place(t1), TILES)
            for u in range(TILE // SUB):
                make(c2, t2, 0, u)
                weigh(c1, spare, 1, u)
            return c2, t2

        lax.fori_loop(0, (total + 1) // 2, pair, (begin, jnp.int32(0)))


def token_of(row):
    return ((row >> 9) & 3) * (2 * QT) + (row >> 11) * QT + ((row >> 4) & (QT - 1))


def live_tiles(tokens, half):
    return half * (HALF // TILE), jnp.clip((tokens - half * QT + 127) // 128, 0, HALF // TILE)


def own_kernel(
    me, placement, hist_len, new_count, q_mine, q_theirs, new_keys, new_values, keys, values,
    q_all, acc, tops, k_all, v_all, counts, score0, score1, found0, found1,
):
    x, z, core = me[0], me[1], me[2]
    for n, shift in enumerate((0, 1, 3, 2)):
        there = (z - shift + 4) % 4
        rows = slice(n * PIECE, (n + 1) * PIECE)
        q_all[rows_at((core * 4 + there) * PIECE, PIECE), :] = q_mine[rows, :]
        q_all[rows_at(((1 - core) * 4 + there) * PIECE, PIECE), :] = q_theirs[rows, :]

    tokens = new_count[x]
    new_first = (z * 2 + core) * QT
    k_all[0:BLK, :] = jnp.zeros((BLK, HD), bf16)
    k_all[0:QT, :] = new_values[...]
    put(k_all, v_all, k_all[0:BLK, :], k_all[0:BLK, :], 0)
    for t in range(ROWS // FIRST):
        at = slice(t * FIRST, (t + 1) * FIRST)
        s = lax.dot_general(new_keys[...], q_all[at, :], BY_HEAD, preferred_element_type=f32)
        offset = lax.broadcasted_iota(i32, (QT, FIRST), 0)
        token = token_of(t * FIRST + lax.broadcasted_iota(i32, (1, FIRST), 1))
        allowed = offset <= jnp.minimum(token, tokens - 1) - new_first
        top = jnp.max(jnp.where(allowed, s, masked_value), axis=0, keepdims=True)
        w = jnp.where(allowed, jnp.exp2((s - top) * SCALE2), 0.0).astype(bf16)
        tops[0:1, at] = top
        acc[:, at] = lax.dot_general(v_all[:, 0:QT], w, BY_KEY, preferred_element_type=f32)

    def own(i, count):
        request, live = block_state(placement, hist_len, i)
        hit = (request == x) & (live > 0)

        @pl.when(hit)
        def _():
            at = rows_at(i * BLK, BLK)
            put(k_all, v_all, keys[at, :], values[at, :], count)

            @pl.when(live < BLK)
            def _():
                trim(k_all, v_all, count, live)

        return count + hit.astype(i32)

    count = lax.fori_loop(0, HERE, own, jnp.int32(0))
    counts[0] = count
    counts[1] = 0
    tiles = live_tiles(tokens, 0), live_tiles(tokens, 1)
    flash(jnp.int32(0), count // CB, tiles, q_all, k_all, v_all, acc, tops, (score0, score1), (found0, found1))


def take(got, slots, last, count, k_all, v_all):
    lane = lax.broadcasted_iota(i32, (STAT, HD), 1)
    units = jnp.zeros((STAT, HD), f32)
    for at, unit in zip((4, 5, 6, 3) if last else (0, 1, 2, 3), (1.0, 32.0, 1024.0, 262144.0)):
        units = jnp.where(lane == at, unit, units)
    units = jnp.where(lax.broadcasted_iota(i32, (STAT, HD), 0) == 0, units, 0.0)
    meta = jnp.sum(got[2 * slots * BLK :, :].astype(f32) * units).astype(i32)
    here, part_at, part, over = meta & 31, (meta >> 5) & 31, (meta >> 10) & 255, meta >> 18

    def two(i, _):
        for n in (2 * i, 2 * i + 1):
            n_at = jnp.minimum(n, slots - 1)
            at = (slots - 1 - n_at if last else n_at) * (2 * BLK)
            put(k_all, v_all, got[rows_at(at, BLK), :], got[rows_at(at + BLK, BLK), :], count + n)
        return 0

    lax.fori_loop(0, (here + 1) // 2, two, 0)

    @pl.when((part > 0) & (part_at < here))
    def _():
        trim(k_all, v_all, count + part_at, part)

    return count + here, over


def near_kernel(
    cap, me, new_count, counts, own_over, q, got1, got3, acc_in, tops_in, k_in, v_in,
    acc, tops, k_all, v_all, counts_out, score0, score1, found0, found1,
):
    begin = counts[0] // CB
    count, over1 = take(got1, cap, False, counts[0], k_all, v_all)
    count, over3 = take(got3, cap, False, count, k_all, v_all)
    counts_out[0] = count
    counts_out[1] = jnp.maximum(own_over[0], jnp.maximum(over1, over3))
    tokens = new_count[me[0]]
    tiles = live_tiles(tokens, 0), live_tiles(tokens, 1)
    flash(begin, count // CB, tiles, q, k_all, v_all, acc, tops, (score0, score1), (found0, found1))


def sums_of(half, tokens, acc, tops):
    live = token_of(half * HALF + lax.broadcasted_iota(i32, (1, HALF), 1)) < tokens
    at = rows_at(half * HALF, HALF)
    top = jnp.where(live, tops[0:1, at] * SCALE, masked_value)
    total = jnp.where(live, acc[HD : HD + 1, at], 0.0)
    for i in range(CHUNKS):
        cut = slice(i * CHUNK, (i + 1) * CHUNK)
        summed = jnp.where(live[:, cut], acc[0:HD, rows_at(half * HALF + i * CHUNK, CHUNK)], 0.0)
        yield i, top[:, cut], total[:, cut], summed


def store(out, i, top, total, summed, flag):
    pad = jnp.zeros((STAT - 7, CHUNK), f32)
    out[i, 0:HD, :] = summed.astype(bf16)
    out[i, HD:, :] = jnp.concatenate(split3(top) + split3(total) + [flag, pad], axis=0).astype(bf16)


def far_kernel(
    relay, me, new_count, counts, q, far1, far3, acc_in, tops_in, k_in, v_in,
    acc, tops, k_all, v_all, out, counts_out, score0, score1, found0, found1,
):
    begin = counts[0] // CB
    count, over1 = take(far1, relay, True, counts[0], k_all, v_all)
    count, over3 = take(far3, relay, True, count, k_all, v_all)
    end = fill(k_all, v_all, count)
    over = jnp.maximum(counts[1], jnp.maximum(over1, over3))
    counts_out[0] = begin
    counts_out[1] = end
    counts_out[2] = over
    tokens = new_count[me[0]]
    half = 1 - me[2]
    tiles = live_tiles(tokens, half), (0, 0)
    flash(begin, end, tiles, q, k_all, v_all, acc, tops, (score0, score1), (found0, found1))
    flag = jnp.full((1, CHUNK), over.astype(f32))
    for i, top, total, summed in sums_of(half, tokens, acc, tops):
        store(out, i, top, total, summed, flag)


def last_kernel(me, new_count, counts, q, k_all, v_all, acc_in, tops_in, acc, tops, score0, score1, found0, found1):
    tiles = live_tiles(new_count[me[0]], me[2]), (0, 0)
    flash(counts[0], counts[1], tiles, q, k_all, v_all, acc, tops, (score0, score1), (found0, found1))


def join_kernel(me, new_count, counts, acc, tops, theirs, out):
    flag = jnp.full((1, CHUNK), counts[2].astype(f32))
    for i, top, total, summed in sums_of(me[2], new_count[me[0]], acc, tops):
        stat = theirs[i, HD:, :].astype(f32)
        top2 = stat[0:1] + stat[1:2] + stat[2:3]
        total2 = stat[3:4] + stat[4:5] + stat[5:6]
        high = jnp.maximum(top, top2)
        keep, keep2 = jnp.exp(top - high), jnp.exp(top2 - high)
        summed = summed * keep + theirs[i, 0:HD, :].astype(f32) * keep2
        store(out, i, high, total * keep + total2 * keep2, summed, jnp.maximum(flag, stat[6:7]))


def merge_kernel(got, out, flag):
    over = jnp.zeros((1, CHUNK), f32)
    for y in range(REQ):
        tops, totals = [], []
        for c in range(PEERS):
            stat = got[c * REQ + y, HD:, :].astype(f32)
            tops.append(stat[0:1] + stat[1:2] + stat[2:3])
            totals.append(stat[3:4] + stat[4:5] + stat[5:6])
            over = jnp.maximum(over, stat[6:7])
        top, total = jnp.concatenate(tops, axis=0), jnp.concatenate(totals, axis=0)
        rescale = jnp.exp(top - jnp.max(top, axis=0, keepdims=True))
        denominator = jnp.sum(rescale * total, axis=0, keepdims=True)
        share = rescale / jnp.maximum(denominator, 1.0)
        numerator = jnp.zeros((HD, CHUNK), f32)
        for c in range(PEERS):
            numerator = numerator + share[c : c + 1, :] * got[c * REQ + y, 0:HD, :].astype(f32)
        out[:, y] = jnp.transpose(numerator).astype(bf16).reshape(CHUNK // QPK, QPK, HD)
    flag[0] = jnp.max(over).astype(i32)


def shifted(x, axis, by):
    peers = lax.axis_size(axis)
    return lax.ppermute(x, axis, [(i, (i + by) % peers) for i in range(peers)])


def params(mib):
    return pltpu.CompilerParams(vmem_limit_bytes=mib * 1024 * 1024)


def gather_queries(q):
    mine = jnp.concatenate([q] + [shifted(q, "z", by) for by in (1, -1, 2)], axis=0)
    return mine, shifted(mine, "core", 1)


WORKING = [pltpu.VMEM((CB * BLK, TILE), f32)] * 2 + [pltpu.VMEM((8, TILE), f32)] * 2


def cost(blocks):
    return pl.CostEstimate(flops=blocks, bytes_accessed=blocks, transcendentals=0)


def run(cap, relay, me, q, new_keys, new_values, keys, values, hist_len, new_count, placement):
    size = 2 * cap * BLK + STAT
    up, down, over = pl.pallas_call(
        functools.partial(pack_kernel, cap, relay),
        out_shape=[jax.ShapeDtypeStruct((size, HD), bf16)] * 2 + [jax.ShapeDtypeStruct((1,), i32)],
        in_specs=[SMEM] * 3 + [VMEM] * 2,
        out_specs=[VMEM] * 2 + [SMEM],
        compiler_params=params(24),
        name="pack",
    )(me, placement, hist_len, keys, values)
    got1, got3 = shifted(up, "x", 1), shifted(down, "x", -1)
    tail = 2 * (cap - relay) * BLK
    queries = gather_queries(q)
    held = (HERE + 2 * cap + 2 * relay + CB) * BLK
    state = [
        jax.ShapeDtypeStruct((AUG, ROWS + TILE), f32),
        jax.ShapeDtypeStruct((8, ROWS + TILE), f32),
        jax.ShapeDtypeStruct((held, HD), bf16),
        jax.ShapeDtypeStruct((AUG, held), bf16),
    ]
    two = jax.ShapeDtypeStruct((2,), i32)
    q, *now, counts = pl.pallas_call(
        own_kernel,
        out_shape=[jax.ShapeDtypeStruct((ROWS, HD), bf16)] + state + [two],
        in_specs=[SMEM] * 4 + [VMEM] * 6,
        out_specs=[VMEM] * 5 + [SMEM],
        scratch_shapes=WORKING,
        compiler_params=params(32),
        cost_estimate=cost(8),
        name="own",
    )(me, placement, hist_len, new_count, *queries, new_keys, new_values, keys, values)
    counts, got1, got3 = lax.optimization_barrier((counts, got1, got3))
    far1, far3 = shifted(got1[tail:], "x", 1), shifted(got3[tail:], "x", -1)
    *now, counts = pl.pallas_call(
        functools.partial(near_kernel, cap),
        out_shape=state + [two],
        in_specs=[SMEM] * 4 + [VMEM] * 7,
        out_specs=[VMEM] * 4 + [SMEM],
        input_output_aliases={7: 0, 8: 1, 9: 2, 10: 3},
        scratch_shapes=WORKING,
        compiler_params=params(32),
        cost_estimate=cost(8),
        name="near",
    )(me, new_count, counts, over, q, got1, got3, *now)
    sums = jax.ShapeDtypeStruct((CHUNKS, CHUNK + STAT, HD), bf16)
    *now, parts, counts = pl.pallas_call(
        functools.partial(far_kernel, relay),
        out_shape=state + [sums, jax.ShapeDtypeStruct((3,), i32)],
        in_specs=[SMEM] * 3 + [VMEM] * 7,
        out_specs=[VMEM] * 5 + [SMEM],
        input_output_aliases={6: 0, 7: 1, 8: 2, 9: 3},
        scratch_shapes=WORKING,
        compiler_params=params(32),
        cost_estimate=cost(4),
        name="far",
    )(me, new_count, counts, q, far1, far3, *now)
    theirs = shifted(parts, "core", 1)
    acc, tops, k_all, v_all = now
    acc, tops = pl.pallas_call(
        last_kernel,
        out_shape=state[0:2],
        in_specs=[SMEM] * 3 + [VMEM] * 5,
        out_specs=[VMEM] * 2,
        input_output_aliases={6: 0, 7: 1},
        scratch_shapes=WORKING,
        compiler_params=params(32),
        cost_estimate=cost(4),
        name="last",
    )(me, new_count, counts, q, k_all, v_all, acc, tops)
    joined = pl.pallas_call(
        join_kernel,
        out_shape=sums,
        in_specs=[SMEM] * 3 + [VMEM] * 3,
        out_specs=VMEM,
        compiler_params=params(32),
        name="join",
    )(me, new_count, counts, acc, tops, theirs)
    moved = lax.all_to_all(joined, ("z", "head"), split_axis=0, concat_axis=0, tiled=True)
    return pl.pallas_call(
        merge_kernel,
        out_shape=[jax.ShapeDtypeStruct((CHUNK // QPK, REQ, QPK, HD), bf16), jax.ShapeDtypeStruct((1,), i32)],
        in_specs=[VMEM],
        out_specs=[VMEM, SMEM],
        compiler_params=params(24),
        name="merge",
    )(moved)


def local(queries, new_keys, new_values, cache_keys, cache_values, hist_len, new_count, placement):
    me = jnp.stack([lax.axis_index(a) for a in ("x", "z", "core")]).astype(i32)
    rows = queries.reshape(PIECE, HD)
    rest = (new_keys[:, 0], new_values[:, 0], cache_keys[:, 0], cache_values[:, 0], hist_len, new_count, placement)
    attended, flag = run(CAP, RELAY, me, rows, *rest)
    return lax.cond(flag[0] > 0, lambda: run(HERE, HERE, me, rows, *rest)[0], lambda: attended)


def solution(mesh):
    fine = Mesh(mesh.devices.reshape(4, 4, 2, 4), ("x", "z", "core", "head"))
    ctx = ("x", "z", "core")
    in_specs = (
        P(ctx, "head", None, None),
        P(ctx, "head", None),
        P(ctx, "head", None),
        P(ctx, "head", None),
        P(ctx, "head", None),
        P(),
        P(),
        P(ctx),
    )
    out_specs = P((*ctx, "head"), None, None, None)
    return jax.shard_map(local, mesh=fine, in_specs=in_specs, out_specs=out_specs, check_vma=False)
```

```python
import functools
import math

import jax
import jax.numpy as jnp
import numpy as np
from jax import lax
from jax.experimental import pallas as pl
from jax.experimental.pallas import tpu as pltpu
from jax.sharding import Mesh, PartitionSpec as P

HD = 128
QPK = 16
REQ = 4
NEW = 256
BLK = 128
QT = 32
HERE = 16
PEERS = 4
PIECE = QT * QPK
ROWS = NEW * QPK
CHUNK = 128
HALF = ROWS // 2
CHUNKS = HALF // CHUNK
STAT = 16
BLOCKS_REQ = 128
CAP = 9
RELAY = 5
TILE = 1024
TILES = ROWS // TILE
SUB = 256
FIRST = 1024
CB = 4
AUG = HD + STAT

masked_value = -1e30
SCALE = 1.0 / math.sqrt(HD)
SCALE2 = SCALE * math.log2(math.e)

VMEM = pl.BlockSpec(memory_space=pltpu.VMEM)
SMEM = pl.BlockSpec(memory_space=pltpu.SMEM)
f32, bf16, i32 = jnp.float32, jnp.bfloat16, jnp.int32


def block_state(placement, hist_len, i):
    logical = placement[i]
    request = logical // BLOCKS_REQ
    live = hist_len[request] - (logical % BLOCKS_REQ) * BLK
    return request, jnp.clip(live, 0, BLK)


def rows_at(first, count):
    return pl.ds(pl.multiple_of(first, BLK), count)


def pack_kernel(cap, relay, me, placement, hist_len, keys, values, up, down, over_out):
    state = []
    count = [jnp.int32(0)] * REQ
    for i in range(HERE):
        request, live = block_state(placement, hist_len, i)
        away = jnp.where(live > 0, (request - me[0] + REQ) % REQ, 0)
        state.append((away, live, [count[d] for d in range(REQ)]))
        count = [count[d] + (away == d).astype(i32) for d in range(REQ)]
    up_room = jnp.minimum(relay, jnp.maximum(cap - count[1], 0))
    down_room = jnp.minimum(relay, jnp.maximum(cap - count[3], 0))
    far_up = jnp.minimum(jnp.maximum((count[2] + 1) // 2, count[2] - down_room), up_room)
    over = (count[1] > cap) | (count[3] > cap) | (count[2] > up_room + down_room)
    over_out[0] = over.astype(i32)
    part = {d: (jnp.int32(0), jnp.int32(0)) for d in ("near up", "near down", "far up", "far down")}
    for i, (away, live, before) in enumerate(state):
        src = slice(i * BLK, (i + 1) * BLK)
        far = away == 2
        goes_up = far & (before[2] < far_up)
        goes_down = far & (before[2] >= far_up)
        far_down = before[2] - far_up
        places = (
            (up, away == 1, before[1], goes_up, before[2], relay),
            (down, away == 3, before[3], goes_down, far_down, down_room),
        )
        for send, near, near_at, far, far_at, room in places:
            slot = jnp.where(near, near_at, cap - 1 - far_at)

            @pl.when((near & (near_at < cap)) | (far & (far_at < room)))
            def _(send=send, slot=slot, src=src):
                send[rows_at(slot * (2 * BLK), BLK), :] = keys[src, :]
                send[rows_at(slot * (2 * BLK) + BLK, BLK), :] = values[src, :]

        partly = live < BLK
        for name, hit, order in (
            ("near up", away == 1, before[1]),
            ("near down", away == 3, before[3]),
            ("far up", goes_up, before[2]),
            ("far down", goes_down, far_down),
        ):
            part[name] = tuple(jnp.where(hit & partly, new, old) for new, old in zip((order, live), part[name]))
    lane = lax.broadcasted_iota(i32, (STAT, HD), 1)
    numbers = (
        (up, jnp.minimum(count[1], cap), "near up", far_up, "far up"),
        (down, jnp.minimum(count[3], cap), "near down", jnp.minimum(count[2] - far_up, down_room), "far down"),
    )
    for send, near, near_name, far, far_name in numbers:
        meta = jnp.zeros((STAT, HD), i32)
        for k, number in enumerate((near, *part[near_name], over.astype(i32), far, *part[far_name])):
            meta = jnp.where(lane == k, number, meta)
        send[2 * cap * BLK :, :] = meta.astype(f32).astype(bf16)


def split3(x):
    hi = x.astype(bf16).astype(f32)
    mid = (x - hi).astype(bf16).astype(f32)
    lo = (x - hi - mid).astype(bf16).astype(f32)
    return [hi, mid, lo]


def put(k_all, v_all, k_block, v_block, slot):
    at = rows_at(slot * BLK, BLK)
    k_all[at, :] = k_block
    v_all[0:HD, at] = jnp.transpose(v_block.astype(f32)).astype(bf16)
    v_all[HD:, at] = jnp.where(lax.broadcasted_iota(i32, (STAT, BLK), 0) == 0, 1.0, 0.0).astype(bf16)


def trim(k_all, v_all, slot, live):
    at = rows_at(slot * BLK, BLK)
    k32 = k_all[at, :].astype(f32)
    k_all[at, :] = jnp.where(lax.broadcasted_iota(i32, (BLK, HD), 0) < live, k32, k32[0:1, :]).astype(bf16)
    v32 = v_all[:, at].astype(f32)
    v_all[:, at] = jnp.where(lax.broadcasted_iota(i32, (AUG, BLK), 1) < live, v32, 0.0).astype(bf16)


def fill(k_all, v_all, count):
    chunks = (count + CB - 1) // CB

    def again(i, _):
        k_all[rows_at(i * BLK, BLK), :] = k_all[rows_at((count - 1) * BLK, BLK), :]
        v_all[:, rows_at(i * BLK, BLK)] = jnp.zeros((AUG, BLK), bf16)
        return 0

    lax.fori_loop(count, chunks * CB, again, 0)
    return chunks


BY_HEAD = (((1,), (1,)), ((), ()))
BY_KEY = (((1,), (0,)), ((), ()))


def flash(begin, end, tiles, q, k_all, v_all, acc, tops, scores, found):
    wide = CB * BLK
    (first0, count0), (first1, count1) = tiles
    total = (end - begin) * (count0 + count1)

    def place(t):
        return jnp.where(t < count0, first0 + t, first1 + t - count0)

    def make(c, t, n, u):
        cut = slice(u * SUB, (u + 1) * SUB)
        s = lax.dot_general(
            k_all[rows_at(c * wide, wide), :],
            q[rows_at(place(t) * TILE + u * SUB, SUB), :],
            BY_HEAD,
            preferred_element_type=f32,
        )
        scores[n][:, cut] = s
        found[n][0:1, cut] = jnp.max(s, axis=0, keepdims=True)

    def weigh(c, t, n, u):
        cut = slice(u * SUB, (u + 1) * SUB)
        at = rows_at(t * TILE + u * SUB, SUB)
        old = tops[0:1, at]
        top = jnp.maximum(old, found[n][0:1, cut])
        w = jnp.exp2((scores[n][:, cut] - top) * SCALE2).astype(bf16)
        keep = jnp.exp2((old - top) * SCALE2)
        tops[0:1, at] = top
        acc[:, at] = acc[:, at] * keep + lax.dot_general(
            v_all[:, rows_at(c * wide, wide)], w, BY_KEY, preferred_element_type=f32
        )

    def after(c, t):
        wrap = t + 1 == count0 + count1
        return jnp.minimum(c + wrap.astype(i32), end - 1), jnp.where(wrap, 0, t + 1)

    @pl.when(total > 0)
    def _():
        for u in range(TILE // SUB):
            make(begin, jnp.int32(0), 0, u)

        def pair(p, now):
            c, t = now
            c1, t1 = after(c, t)
            c2, t2 = after(c1, t1)
            for u in range(TILE // SUB):
                make(c1, t1, 1, u)
                weigh(c, place(t), 0, u)
            spare = jnp.where(2 * p + 1 < total, place(t1), TILES)
            for u in range(TILE // SUB):
                make(c2, t2, 0, u)
                weigh(c1, spare, 1, u)
            return c2, t2

        lax.fori_loop(0, (total + 1) // 2, pair, (begin, jnp.int32(0)))


def token_of(row):
    return ((row >> 9) & 3) * (2 * QT) + (row >> 11) * QT + ((row >> 4) & (QT - 1))


def live_tiles(tokens, half):
    return half * (HALF // TILE), jnp.clip((tokens - half * QT + 127) // 128, 0, HALF // TILE)


def begin(half, me, new_count, pieces, new_keys, q_all, v_all, acc, tops):
    z, core = me[1], me[2]
    for n, shift in enumerate((0, 1, 3, 2)):
        there = (z - shift + 4) % 4
        q_all[rows_at((half * 4 + there) * PIECE, PIECE), :] = pieces[n * PIECE : (n + 1) * PIECE, :]
    tokens = new_count[me[0]]
    new_first = (z * 2 + core) * QT
    fresh = v_all.shape[1] - BLK
    for t in range(HALF // FIRST):
        at = rows_at(half * HALF + t * FIRST, FIRST)
        s = lax.dot_general(new_keys[...], q_all[at, :], BY_HEAD, preferred_element_type=f32)
        offset = lax.broadcasted_iota(i32, (QT, FIRST), 0)
        token = token_of(half * HALF + t * FIRST + lax.broadcasted_iota(i32, (1, FIRST), 1))
        allowed = offset <= jnp.minimum(token, tokens - 1) - new_first
        top = jnp.max(jnp.where(allowed, s, masked_value), axis=0, keepdims=True)
        w = jnp.where(allowed, jnp.exp2((s - top) * SCALE2), 0.0).astype(bf16)
        tops[0:1, at] = top
        acc[:, at] = lax.dot_general(v_all[:, fresh : fresh + QT], w, BY_KEY, preferred_element_type=f32)
    return live_tiles(tokens, half), (0, 0)


def own_kernel(
    me, placement, hist_len, new_count, q_mine, new_keys, new_values, keys, values,
    q_all, acc, tops, k_all, v_all, counts, score0, score1, found0, found1,
):
    x, core = me[0], me[2]
    fresh = k_all.shape[0] - BLK
    k_all[fresh:, :] = jnp.zeros((BLK, HD), bf16)
    k_all[fresh : fresh + QT, :] = new_values[...]
    put(k_all, v_all, k_all[fresh:, :], k_all[fresh:, :], fresh // BLK)
    tiles = begin(core, me, new_count, q_mine, new_keys, q_all, v_all, acc, tops)

    def own(i, count):
        request, live = block_state(placement, hist_len, i)
        hit = (request == x) & (live > 0)

        @pl.when(hit)
        def _():
            at = rows_at(i * BLK, BLK)
            put(k_all, v_all, keys[at, :], values[at, :], count)

            @pl.when(live < BLK)
            def _():
                trim(k_all, v_all, count, live)

        return count + hit.astype(i32)

    count = lax.fori_loop(0, HERE, own, jnp.int32(0))
    counts[0] = count
    counts[1] = 0
    flash(jnp.int32(0), count // CB, tiles, q_all, k_all, v_all, acc, tops, (score0, score1), (found0, found1))


def other_kernel(
    me, new_count, counts, q_theirs, new_keys, q_in, acc_in, tops_in, k_all, v_all,
    q_all, acc, tops, score0, score1, found0, found1,
):
    tiles = begin(1 - me[2], me, new_count, q_theirs, new_keys, q_all, v_all, acc, tops)
    flash(jnp.int32(0), counts[0] // CB, tiles, q_all, k_all, v_all, acc, tops, (score0, score1), (found0, found1))


def take(got, slots, last, count, k_all, v_all):
    lane = lax.broadcasted_iota(i32, (STAT, HD), 1)
    units = jnp.zeros((STAT, HD), f32)
    for at, unit in zip((4, 5, 6, 3) if last else (0, 1, 2, 3), (1.0, 32.0, 1024.0, 262144.0)):
        units = jnp.where(lane == at, unit, units)
    units = jnp.where(lax.broadcasted_iota(i32, (STAT, HD), 0) == 0, units, 0.0)
    meta = jnp.sum(got[2 * slots * BLK :, :].astype(f32) * units).astype(i32)
    here, part_at, part, over = meta & 31, (meta >> 5) & 31, (meta >> 10) & 255, meta >> 18

    def two(i, _):
        for n in (2 * i, 2 * i + 1):
            n_at = jnp.minimum(n, slots - 1)
            at = (slots - 1 - n_at if last else n_at) * (2 * BLK)
            put(k_all, v_all, got[rows_at(at, BLK), :], got[rows_at(at + BLK, BLK), :], count + n)
        return 0

    lax.fori_loop(0, (here + 1) // 2, two, 0)

    @pl.when((part > 0) & (part_at < here))
    def _():
        trim(k_all, v_all, count + part_at, part)

    return count + here, over


def near_kernel(
    cap, me, new_count, counts, own_over, q, got1, got3, acc_in, tops_in, k_in, v_in,
    acc, tops, k_all, v_all, counts_out, score0, score1, found0, found1,
):
    begin = counts[0] // CB
    count, over1 = take(got1, cap, False, counts[0], k_all, v_all)
    count, over3 = take(got3, cap, False, count, k_all, v_all)
    counts_out[0] = count
    counts_out[1] = jnp.maximum(own_over[0], jnp.maximum(over1, over3))
    tokens = new_count[me[0]]
    tiles = live_tiles(tokens, 0), live_tiles(tokens, 1)
    flash(begin, count // CB, tiles, q, k_all, v_all, acc, tops, (score0, score1), (found0, found1))


def sums_of(half, tokens, acc, tops):
    live = token_of(half * HALF + lax.broadcasted_iota(i32, (1, HALF), 1)) < tokens
    at = rows_at(half * HALF, HALF)
    top = jnp.where(live, tops[0:1, at] * SCALE, masked_value)
    total = jnp.where(live, acc[HD : HD + 1, at], 0.0)
    for i in range(CHUNKS):
        cut = slice(i * CHUNK, (i + 1) * CHUNK)
        summed = jnp.where(live[:, cut], acc[0:HD, rows_at(half * HALF + i * CHUNK, CHUNK)], 0.0)
        yield i, top[:, cut], total[:, cut], summed


def store(out, i, top, total, summed, flag):
    pad = jnp.zeros((STAT - 7, CHUNK), f32)
    out[i, 0:HD, :] = summed.astype(bf16)
    out[i, HD:, :] = jnp.concatenate(split3(top) + split3(total) + [flag, pad], axis=0).astype(bf16)


def far_kernel(
    relay, me, new_count, counts, q, far1, far3, acc_in, tops_in, k_in, v_in,
    acc, tops, k_all, v_all, out, counts_out, score0, score1, found0, found1,
):
    begin = counts[0] // CB
    count, over1 = take(far1, relay, True, counts[0], k_all, v_all)
    count, over3 = take(far3, relay, True, count, k_all, v_all)
    end = fill(k_all, v_all, count)
    over = jnp.maximum(counts[1], jnp.maximum(over1, over3))
    counts_out[0] = begin
    counts_out[1] = end
    counts_out[2] = over
    tokens = new_count[me[0]]
    half = 1 - me[2]
    tiles = live_tiles(tokens, half), (0, 0)
    flash(begin, end, tiles, q, k_all, v_all, acc, tops, (score0, score1), (found0, found1))
    flag = jnp.full((1, CHUNK), over.astype(f32))
    for i, top, total, summed in sums_of(half, tokens, acc, tops):
        store(out, i, top, total, summed, flag)


def last_kernel(me, new_count, counts, q, k_all, v_all, acc_in, tops_in, acc, tops, score0, score1, found0, found1):
    tiles = live_tiles(new_count[me[0]], me[2]), (0, 0)
    flash(counts[0], counts[1], tiles, q, k_all, v_all, acc, tops, (score0, score1), (found0, found1))


def join_kernel(me, new_count, counts, acc, tops, theirs, out):
    flag = jnp.full((1, CHUNK), counts[2].astype(f32))
    for i, top, total, summed in sums_of(me[2], new_count[me[0]], acc, tops):
        stat = theirs[i, HD:, :].astype(f32)
        top2 = stat[0:1] + stat[1:2] + stat[2:3]
        total2 = stat[3:4] + stat[4:5] + stat[5:6]
        high = jnp.maximum(top, top2)
        keep, keep2 = jnp.exp(top - high), jnp.exp(top2 - high)
        summed = summed * keep + theirs[i, 0:HD, :].astype(f32) * keep2
        store(out, i, high, total * keep + total2 * keep2, summed, jnp.maximum(flag, stat[6:7]))


def merge_kernel(got, out, flag):
    over = jnp.zeros((1, CHUNK), f32)
    for y in range(REQ):
        tops, totals = [], []
        for c in range(PEERS):
            stat = got[c * REQ + y, HD:, :].astype(f32)
            tops.append(stat[0:1] + stat[1:2] + stat[2:3])
            totals.append(stat[3:4] + stat[4:5] + stat[5:6])
            over = jnp.maximum(over, stat[6:7])
        top, total = jnp.concatenate(tops, axis=0), jnp.concatenate(totals, axis=0)
        rescale = jnp.exp(top - jnp.max(top, axis=0, keepdims=True))
        denominator = jnp.sum(rescale * total, axis=0, keepdims=True)
        share = rescale / jnp.maximum(denominator, 1.0)
        numerator = jnp.zeros((HD, CHUNK), f32)
        for c in range(PEERS):
            numerator = numerator + share[c : c + 1, :] * got[c * REQ + y, 0:HD, :].astype(f32)
        out[:, y] = jnp.transpose(numerator).astype(bf16).reshape(CHUNK // QPK, QPK, HD)
    flag[0] = jnp.max(over).astype(i32)


def shifted(x, axis, by):
    peers = lax.axis_size(axis)
    return lax.ppermute(x, axis, [(i, (i + by) % peers) for i in range(peers)])


def params(mib):
    return pltpu.CompilerParams(vmem_limit_bytes=mib * 1024 * 1024)


def gather_queries(q):
    mine = jnp.concatenate([q] + [shifted(q, "z", by) for by in (1, -1, 2)], axis=0)
    return mine, shifted(mine, "core", 1)


WORKING = [pltpu.VMEM((CB * BLK, TILE), f32)] * 2 + [pltpu.VMEM((8, TILE), f32)] * 2


def cost(blocks):
    return pl.CostEstimate(flops=blocks, bytes_accessed=blocks, transcendentals=0)


def run(cap, relay, me, q, new_keys, new_values, keys, values, hist_len, new_count, placement):
    size = 2 * cap * BLK + STAT
    up, down, over = pl.pallas_call(
        functools.partial(pack_kernel, cap, relay),
        out_shape=[jax.ShapeDtypeStruct((size, HD), bf16)] * 2 + [jax.ShapeDtypeStruct((1,), i32)],
        in_specs=[SMEM] * 3 + [VMEM] * 2,
        out_specs=[VMEM] * 2 + [SMEM],
        compiler_params=params(24),
        name="pack",
    )(me, placement, hist_len, keys, values)
    got1, got3 = shifted(up, "x", 1), shifted(down, "x", -1)
    tail = 2 * (cap - relay) * BLK
    queries = gather_queries(q)
    held = (HERE + 2 * cap + 2 * relay + CB + 1) * BLK
    state = [
        jax.ShapeDtypeStruct((AUG, ROWS + TILE), f32),
        jax.ShapeDtypeStruct((8, ROWS + TILE), f32),
        jax.ShapeDtypeStruct((held, HD), bf16),
        jax.ShapeDtypeStruct((AUG, held), bf16),
    ]
    two = jax.ShapeDtypeStruct((2,), i32)
    rows = jax.ShapeDtypeStruct((ROWS, HD), bf16)
    q_mine, q_theirs = queries
    q, acc, tops, k_all, v_all, counts = pl.pallas_call(
        own_kernel,
        out_shape=[rows] + state + [two],
        in_specs=[SMEM] * 4 + [VMEM] * 5,
        out_specs=[VMEM] * 5 + [SMEM],
        scratch_shapes=WORKING,
        compiler_params=params(32),
        cost_estimate=cost(8),
        name="own",
    )(me, placement, hist_len, new_count, q_mine, new_keys, new_values, keys, values)
    counts, got1, got3 = lax.optimization_barrier((counts, got1, got3))
    q, acc, tops = pl.pallas_call(
        other_kernel,
        out_shape=[rows] + state[0:2],
        in_specs=[SMEM] * 3 + [VMEM] * 7,
        out_specs=[VMEM] * 3,
        input_output_aliases={5: 0, 6: 1, 7: 2},
        scratch_shapes=WORKING,
        compiler_params=params(32),
        cost_estimate=cost(8),
        name="other",
    )(me, new_count, counts, q_theirs, new_keys, q, acc, tops, k_all, v_all)
    now = [acc, tops, k_all, v_all]
    far1, far3 = shifted(got1[tail:], "x", 1), shifted(got3[tail:], "x", -1)
    *now, counts = pl.pallas_call(
        functools.partial(near_kernel, cap),
        out_shape=state + [two],
        in_specs=[SMEM] * 4 + [VMEM] * 7,
        out_specs=[VMEM] * 4 + [SMEM],
        input_output_aliases={7: 0, 8: 1, 9: 2, 10: 3},
        scratch_shapes=WORKING,
        compiler_params=params(32),
        cost_estimate=cost(8),
        name="near",
    )(me, new_count, counts, over, q, got1, got3, *now)
    sums = jax.ShapeDtypeStruct((CHUNKS, CHUNK + STAT, HD), bf16)
    *now, parts, counts = pl.pallas_call(
        functools.partial(far_kernel, relay),
        out_shape=state + [sums, jax.ShapeDtypeStruct((3,), i32)],
        in_specs=[SMEM] * 3 + [VMEM] * 7,
        out_specs=[VMEM] * 5 + [SMEM],
        input_output_aliases={6: 0, 7: 1, 8: 2, 9: 3},
        scratch_shapes=WORKING,
        compiler_params=params(32),
        cost_estimate=cost(4),
        name="far",
    )(me, new_count, counts, q, far1, far3, *now)
    theirs = shifted(parts, "core", 1)
    acc, tops, k_all, v_all = now
    acc, tops = pl.pallas_call(
        last_kernel,
        out_shape=state[0:2],
        in_specs=[SMEM] * 3 + [VMEM] * 5,
        out_specs=[VMEM] * 2,
        input_output_aliases={6: 0, 7: 1},
        scratch_shapes=WORKING,
        compiler_params=params(32),
        cost_estimate=cost(4),
        name="last",
    )(me, new_count, counts, q, k_all, v_all, acc, tops)
    joined = pl.pallas_call(
        join_kernel,
        out_shape=sums,
        in_specs=[SMEM] * 3 + [VMEM] * 3,
        out_specs=VMEM,
        compiler_params=params(32),
        name="join",
    )(me, new_count, counts, acc, tops, theirs)
    moved = lax.all_to_all(joined, ("z", "head"), split_axis=0, concat_axis=0, tiled=True)
    return pl.pallas_call(
        merge_kernel,
        out_shape=[jax.ShapeDtypeStruct((CHUNK // QPK, REQ, QPK, HD), bf16), jax.ShapeDtypeStruct((1,), i32)],
        in_specs=[VMEM],
        out_specs=[VMEM, SMEM],
        compiler_params=params(24),
        name="merge",
    )(moved)


def local(queries, new_keys, new_values, cache_keys, cache_values, hist_len, new_count, placement):
    me = jnp.stack([lax.axis_index(a) for a in ("x", "z", "core")]).astype(i32)
    rows = queries.reshape(PIECE, HD)
    rest = (new_keys[:, 0], new_values[:, 0], cache_keys[:, 0], cache_values[:, 0], hist_len, new_count, placement)
    attended, flag = run(CAP, RELAY, me, rows, *rest)
    return lax.cond(flag[0] > 0, lambda: run(HERE, HERE, me, rows, *rest)[0], lambda: attended)


def solution(mesh):
    fine = Mesh(mesh.devices.reshape(4, 4, 2, 4), ("x", "z", "core", "head"))
    ctx = ("x", "z", "core")
    in_specs = (
        P(ctx, "head", None, None),
        P(ctx, "head", None),
        P(ctx, "head", None),
        P(ctx, "head", None),
        P(ctx, "head", None),
        P(),
        P(),
        P(ctx),
    )
    out_specs = P((*ctx, "head"), None, None, None)
    return jax.shard_map(local, mesh=fine, in_specs=in_specs, out_specs=out_specs, check_vma=False)
```
